1024 devices in a mesh: dp: 64 (over z, x), tensor: 16 (over y, core).
Axes of the slice: x: 8, y: 8, z: 8, core: 2. Of those that a mesh axis runs over, the one named last changes fastest.
Arguments:
- masters: float32 [16, 64, 38400], P('tensor', 'dp'), may hold values from -0.078125 to 0.078125
- offsets: int32 [65], replicated, may hold values from 0 to 1638400, as said below
- tokens: bfloat16 [2, 64, 64, 5120], P(None, 'dp'), may hold values from -6 to 6
- lengths: int32 [64, 64], P('dp'), may hold values from 2 to 256, as said below
- cache_keys: bfloat16 [64, 16, 16, 256, 128], P('dp', 'tensor')
- cache_values: bfloat16 [64, 16, 16, 256, 128], P('dp', 'tensor'), may hold values from -6 to 6
Outputs:
- attended: bfloat16 [2, 64, 16, 16, 1024], P(None, 'dp', 'tensor')
- new_entries: bfloat16 [2, 64, 16, 16, 256], P(None, 'dp', 'tensor')
The draws below stay inside these ranges and needn't reach their ends.
Inputs may be any that keep to these rules, and one draw needn't show every extreme that they name: offsets[0] = 0 and offsets[64] = 1638400; every offset is a multiple of 128; offsets[p] lies within 6400 of p * 25600; in every draw some piece is exactly 38400 long. `lengths`: in every group some row has exactly 256 cached positions.
All inputs are finite; a program needn't handle non-finite values.
Results may differ from the reference program's by a relative error of at most 0.011.
Values may be sent and summed in bfloat16 or wider, within the bound.
A program may use at most 32 MiB of HBM per device.

```python
import math
import jax
import jax.numpy as jnp
from jax import lax

D = 5120
HD = 128
QH_DEV = 2
GQ = 8
GRAIN = 128
ROWS_Q = 16
L = 256
HEADS = 32
KVH = 4
GROUP_ROWS = 64
PIECE = 25600
CAP = 38400
N_DP = 64
N_TENSOR = 16


def draw_offsets(key, part):
    key = jax.random.fold_in(key, 11)
    shift_key, pick_key = jax.random.split(key)
    margin = PIECE // 4 // GRAIN
    shifts = jax.random.randint(shift_key, (N_DP + 1,), -margin, margin + 1)
    chosen = jax.random.randint(pick_key, (), 1, N_DP - 1)
    places = jnp.arange(N_DP + 1, dtype=jnp.int32)
    shifts = jnp.where(places == chosen, -margin, shifts)
    shifts = jnp.where(places == chosen + 1, margin, shifts)
    shifts = jnp.where((places == 0) | (places == N_DP), 0, shifts)
    return (places * PIECE + shifts * GRAIN).astype(jnp.int32)


def draw_lengths(key, part):
    key = jax.random.fold_in(key, 7)
    base_key, pick_key = jax.random.split(key)
    row_lengths = jax.random.randint(base_key, (N_DP, GROUP_ROWS), 2, L + 1)
    longest = jax.random.randint(pick_key, (N_DP, 1), 0, GROUP_ROWS)
    columns = jnp.arange(GROUP_ROWS, dtype=jnp.int32)[None, :]
    return jnp.where(columns == longest, L, row_lengths).astype(jnp.int32)


def draw_cache_keys(key, part):
    key = jax.random.fold_in(key, 5)
    base_key = jax.random.fold_in(key, 0)
    full_shape = (N_DP, N_TENSOR, ROWS_Q, L, HD)
    base = jax.random.normal(base_key, full_shape, jnp.float32)
    return base.astype(jnp.bfloat16)


def block_levels(key, extent, cuts, smallest, largest):
    factor_of, own = 1.0, jax.random.fold_in(key, 6)
    for axis_at, shards_of in cuts:
        heights = jnp.exp(jax.random.uniform(jax.random.fold_in(own, axis_at), (shards_of,), jnp.float32, smallest / len(cuts), largest / len(cuts)))
        factor_of = factor_of * jnp.repeat(heights, extent[axis_at] // shards_of).reshape([-1 if axis == axis_at else 1 for axis in range(len(extent))])
    return factor_of


def scatter_about(stream_key, extent, spread, limit, cuts=(), held_as=jnp.bfloat16):
    array = spread * jax.random.normal(stream_key, extent, jnp.float32)
    if cuts:
        array = array * block_levels(stream_key, extent, cuts, -0.22, 0.18)
    return jnp.clip(array, -limit, limit).astype(held_as)


def setup_inputs(seed: int = 0) -> dict:
    splits = jax.random.split(jax.random.key(seed), 7)
    return {
        "masters": scatter_about(splits[0], (N_TENSOR, N_DP, CAP), D ** -0.5, 0.078125, ((0, 16), (1, 64)), jnp.float32),
        "offsets": draw_offsets(jax.random.fold_in(splits[6], 71), 0),
        "tokens": scatter_about(splits[2], (2, N_DP, GROUP_ROWS, D), 1.0, 6.0, ((1, 64),)),
        "lengths": draw_lengths(jax.random.fold_in(splits[6], 71), 0),
        "cache_keys": draw_cache_keys(jax.random.fold_in(splits[6], 71), 0),
        "cache_values": scatter_about(splits[5], (N_DP, N_TENSOR, ROWS_Q, L, HD), 1.0, 6.0, ((0, 64), (1, 16))),
    }


ROPE_BASE = 1000000.0


def rotate(values, positions, freq_index):
    half = values.shape[-1] // 2
    inverse = jnp.exp(freq_index.astype(jnp.float32) * (-2.0 * math.log(ROPE_BASE) / HD))
    angles = positions * inverse
    cosine = jnp.cos(angles)
    sine_part = jnp.sin(angles)
    leading = values[..., :half]
    trailing = values[..., half:]
    return jnp.concatenate([leading * cosine - trailing * sine_part, trailing * cosine + leading * sine_part], axis=-1)


def unpack(master, offsets):
    entry_count = D * (QH_DEV * HD + HD // 2)
    entries = jnp.arange(entry_count, dtype=jnp.int32)
    owner_index = jnp.clip(jnp.searchsorted(offsets, entries, side="right").astype(jnp.int32) - 1, 0, N_DP - 1)
    within = entries - offsets[owner_index]
    return master.reshape(-1)[owner_index * CAP + within].astype(jnp.bfloat16)


def attend(queries, keys, values, new_keys, new_values, row_lengths):
    score_scale = HD ** -0.5
    query_wide = queries.astype(jnp.float32)
    cache_scores = jnp.einsum("stigh,tilh->stigl", query_wide, keys.astype(jnp.float32)) * score_scale
    live_mask = jnp.arange(keys.shape[2], dtype=jnp.int32)[None, None, :] < row_lengths[:, :, None]
    cache_scores = jnp.where(live_mask[None, :, :, None, :], cache_scores, -jnp.inf)
    own_scores = jnp.einsum("stigh,jtih->stigj", query_wide, new_keys.astype(jnp.float32)) * score_scale
    allowed = jnp.arange(2, dtype=jnp.int32)[None, :] <= jnp.arange(2, dtype=jnp.int32)[:, None]
    own_scores = jnp.where(allowed[:, None, None, None, :], own_scores, -jnp.inf)
    row_top = jnp.maximum(jnp.max(cache_scores, axis=-1, keepdims=True), jnp.max(own_scores, axis=-1, keepdims=True))
    cache_exp = jnp.exp(cache_scores - row_top)
    own_exp = jnp.exp(own_scores - row_top)
    denominator = jnp.sum(cache_exp, axis=-1, keepdims=True) + jnp.sum(own_exp, axis=-1, keepdims=True)
    cache_weights = (cache_exp / denominator).astype(jnp.bfloat16)
    own_weights = (own_exp / denominator).astype(jnp.bfloat16)
    mixed = jnp.einsum("stigl,tilh->stigh", cache_weights.astype(jnp.float32), values.astype(jnp.float32))
    mixed = mixed + jnp.einsum("stigj,jtih->stigh", own_weights.astype(jnp.float32), new_values.astype(jnp.float32))
    return mixed.astype(jnp.bfloat16)


def reference(masters, offsets, tokens, lengths, cache_keys, cache_values):
    flat_weights = lax.map(lambda master: unpack(master, offsets), masters)
    query_width = QH_DEV * HD
    split_at = D * query_width
    query_weight = flat_weights[:, :split_at].reshape(N_TENSOR, D, query_width)
    query_weight = query_weight.transpose(1, 0, 2).reshape(D, N_TENSOR * query_width).astype(jnp.float32)
    quarter_weight = flat_weights[:, split_at:].reshape(N_TENSOR, 2, D, HD // 4).astype(jnp.float32)
    freq_query = jnp.arange(HD // 2, dtype=jnp.int32)
    freq_quarter = (jnp.arange(N_TENSOR, dtype=jnp.int32) % 4)[:, None] * (HD // 8) + jnp.arange(HD // 8, dtype=jnp.int32)[None, :]

    def one_group(group):
        inputs, row_lengths, keys, values = group
        positions = (row_lengths[None, :] + jnp.arange(2, dtype=jnp.int32)[:, None]).astype(jnp.float32)
        projected = jnp.einsum("srd,dc->src", inputs.astype(jnp.float32), query_weight)
        projected = projected.reshape(2, GROUP_ROWS, HEADS, HD)
        queries = rotate(projected, positions[:, :, None, None], freq_query).astype(jnp.bfloat16)
        quarters = jnp.einsum("srd,tkdc->srtkc", inputs.astype(jnp.float32), quarter_weight)
        rotated = rotate(quarters[:, :, :, 0, :], positions[:, :, None, None], freq_quarter)
        quarters = jnp.stack([rotated, quarters[:, :, :, 1, :]], axis=3).astype(jnp.bfloat16)
        entries = quarters.reshape(2, GROUP_ROWS, KVH, 4, 2, 2, HD // 8).transpose(0, 1, 2, 4, 5, 3, 6)
        entries = entries.reshape(2, 4, ROWS_Q, KVH, 2, HD).transpose(0, 3, 1, 2, 4, 5).reshape(2, N_TENSOR, ROWS_Q, 2, HD)
        queries = queries.reshape(2, 4, ROWS_Q, KVH, GQ, HD).transpose(0, 3, 1, 2, 4, 5).reshape(2, N_TENSOR, ROWS_Q, GQ, HD)
        device_lengths = jnp.broadcast_to(row_lengths.reshape(1, 4, ROWS_Q), (KVH, 4, ROWS_Q)).reshape(N_TENSOR, ROWS_Q)
        mixed = attend(queries, keys, values, entries[:, :, :, 0, :], entries[:, :, :, 1, :], device_lengths)
        return mixed.reshape(2, N_TENSOR, ROWS_Q, GQ * HD), entries.reshape(2, N_TENSOR, ROWS_Q, 2 * HD)

    attended, new_entries = lax.map(one_group, (tokens.transpose(1, 0, 2, 3), lengths, cache_keys, cache_values))
    return attended.transpose(1, 0, 2, 3, 4), new_entries.transpose(1, 0, 2, 3, 4)
```

```python
import math

import jax
import jax.numpy as jnp
from jax import lax
from jax.experimental import pallas as pl
from jax.experimental.pallas import tpu as pltpu
from jax.sharding import PartitionSpec as P

D = 5120
HD = 128
GRAIN = 128
SIDE = 8
UNIT = 32
SLAB = 50
HALF = SLAB // 2
QUERY_UNITS = 320
KEY_UNITS = 40
ROWS = 128
FRONT = 144
ROPE_BASE = 1000000.0
MESH = pl.DeviceIdType.MESH
F32 = jnp.float32
BF16 = jnp.bfloat16
NEAR_FIRST = (1, 7, 2, 6, 3, 5, 4)


def remote(src, dst, send_sem, recv_sem, device):
    return pltpu.make_async_remote_copy(
        src_ref=src, dst_ref=dst, send_sem=send_sem, recv_sem=recv_sem, device_id=device, device_id_type=MESH
    )


def wrap(value):
    return lax.rem(value + 2 * SIDE, SIDE)


def first_unit(x):
    return 6 * x + x // 4


def either(wide, act):
    @pl.when(wide)
    def _():
        act(7)

    @pl.when(jnp.logical_not(wide))
    def _():
        act(6)


def lanes_of(shape):
    return lax.broadcasted_iota(jnp.int32, shape, len(shape) - 1)


def rows_of(shape):
    return lax.broadcasted_iota(jnp.int32, shape, len(shape) - 2)


def kernel(
    masters,
    offsets,
    tokens_in,
    lengths,
    keys_in,
    values_in,
    attended,
    new_entries,
    raw,
    staged,
    from_below,
    from_above,
    ga,
    gb,
    tokens,
    keys,
    values,
    thinned,
    position,
    tables,
    outbox,
    inbox,
    queries,
    mixed,
    load_sem,
    near_send,
    near_recv,
    light_send,
    light_recv,
    ring_send,
    ring_recv,
    swap_send,
    swap_recv,
):
    dp = lax.axis_index("dp")
    t = lax.axis_index("tensor")
    z, x = dp // SIDE, lax.rem(dp, SIDE)
    quarter = lax.rem(t, 4)
    t_base = t - quarter

    loads = [
        pltpu.make_async_copy(masters, raw.at[pl.ds(FRONT, 300)], load_sem.at[0]),
        pltpu.make_async_copy(tokens_in, tokens, load_sem.at[1]),
        pltpu.make_async_copy(keys_in, keys, load_sem.at[2]),
        pltpu.make_async_copy(values_in, values, load_sem.at[3]),
    ]
    for load in loads:
        load.start()

    barrier = pltpu.get_barrier_semaphore()
    for step in range(1, SIDE):
        pl.semaphore_signal(barrier, inc=1, device_id=(z * SIDE + wrap(x + step), t), device_id_type=MESH)
        pl.semaphore_signal(barrier, inc=1, device_id=(wrap(z + step) * SIDE + x, t), device_id_type=MESH)
    for step in range(1, 4):
        pl.semaphore_signal(barrier, inc=1, device_id=(dp, t_base + lax.rem(quarter + step, 4)), device_id_type=MESH)

    @pl.when(dp > 0)
    def _():
        pl.semaphore_signal(barrier, inc=1, device_id=(dp - 1, t), device_id_type=MESH)

    @pl.when(dp < 63)
    def _():
        pl.semaphore_signal(barrier, inc=1, device_id=(dp + 1, t), device_id_type=MESH)

    wide = lax.rem(x, 4) == 3
    count = jnp.where(wide, 7, 6)
    base = z * SLAB + first_unit(x)
    own_start = offsets[dp] // GRAIN
    own_end = offsets[dp + 1] // GRAIN
    raw[0:FRONT] = jnp.zeros((FRONT, GRAIN), F32)
    raw[FRONT + 300 : 528] = jnp.zeros((528 - FRONT - 300, GRAIN), F32)
    loads[0].wait()
    for w in range(12):
        begin = jnp.clip(FRONT + UNIT * (base - 2 + w) - own_start, 0, 494)
        for odd in range(2):
            staged[w, odd] = raw[pl.ds(begin + odd, 16, stride=2), :].astype(BF16)

    pl.semaphore_wait(barrier, 2 * (SIDE - 1) + 3 + jnp.where(dp > 0, 1, 0) + jnp.where(dp < 63, 1, 0))

    up = remote(
        staged.at[pl.ds(2 + count, 3)], from_below, near_send.at[0], near_recv.at[0], (jnp.minimum(dp + 1, 63), t)
    )
    down = remote(staged.at[pl.ds(0, 2)], from_above, near_send.at[1], near_recv.at[1], (jnp.maximum(dp - 1, 0), t))

    @pl.when(dp < 63)
    def _():
        up.start()

    @pl.when(dp > 0)
    def _():
        down.start()

    @pl.when(dp > 0)
    def _():
        up.wait_recv()

    @pl.when(dp < 63)
    def _():
        down.wait_recv()

    def settle(i):
        for odd, target in ((0, ga), (1, gb)):
            row = UNIT * (base + i) + odd + 2 * rows_of((16, GRAIN))
            entry = staged[2 + i, odd].astype(F32)
            if i < 3:
                entry = jnp.where(row < own_start, from_below[i, odd].astype(F32), entry)
            if i > 3:
                place = jnp.clip(i - count + 2, 0, 1)
                entry = jnp.where(row >= own_end, from_above[place, odd].astype(F32), entry)
            target[z, first_unit(x) + i] = entry.astype(BF16)

    for i in range(6):
        settle(i)

    @pl.when(wide)
    def _():
        settle(6)

    def piece(ref, at_z, at_x, n):
        return ref.at[at_z, pl.ds(first_unit(at_x), n)]

    def light(which, step, n, sending):
        if which == 0:
            other = wrap(x + step)
            at_x = x if sending else wrap(x - step)
            ref = piece(ga, z, at_x, n)
            device = (z * SIDE + other, t)
        else:
            at_z = z if sending else wrap(z - step)
            ref = piece(gb, at_z, x, n)
            device = (wrap(z + step) * SIDE + x, t)
        return remote(ref, ref, light_send.at[which, step], light_recv.at[which, step], device)

    def neighbour(which, way):
        move = 1 if way == 0 else -1
        return (wrap(z + move) * SIDE + x, t) if which == 0 else (z * SIDE + wrap(x + move), t)

    def spread(which, at, n):
        for way in range(2):
            ref = piece(ga, z, at, n) if which == 0 else piece(gb, at, x, n)
            remote(
                ref, ref, ring_send.at[which, way, 0, 0], ring_recv.at[which, way, 0, at // 4], neighbour(which, way)
            ).start()

    def send_own(n):
        spread(0, x, n)
        spread(1, z, n)
        for step in NEAR_FIRST:
            light(0, step, n, True).start()
            light(1, step, n, True).start()

    either(wide, send_own)

    for r in range(64):
        here = jnp.full((1, HD), lengths[0, r], jnp.int32).astype(F32)
        position[r : r + 1] = here
        position[64 + r : 65 + r] = here + 1.0
    lane = lanes_of((ROWS, HD))
    rate = -2.0 * math.log(ROPE_BASE) / HD
    angle = position[...] * jnp.exp(lax.rem(lane, 64).astype(F32) * rate)
    tables[0] = jnp.cos(angle)
    tables[1] = jnp.where(lane < 64, -1.0, 1.0) * jnp.sin(angle)
    angle = position[...] * jnp.exp((quarter * 16 + lax.rem(lane, 16)).astype(F32) * rate)
    tables[2] = jnp.cos(angle)
    tables[3] = jnp.where(lax.rem(lane, 32) < 16, -1.0, 1.0) * jnp.sin(angle)

    for step in NEAR_FIRST:
        at_x = wrap(x - step)

        def pass_a(n):
            light(0, step, n, False).wait_recv()
            spread(0, at_x, n)

        def pass_b(n):
            light(1, step, n, False).wait_recv()
            spread(1, wrap(z - step), n)

        either(lax.rem(at_x, 4) == 3, pass_a)
        either(wide, pass_b)

    loads[1].wait()

    def thin(e):
        pick = (rows_of((1024, HD)) == 8 * lanes_of((1024, HD)) + e).astype(F32).astype(BF16)
        for block in range(D // 1024):
            got = jnp.dot(tokens[:, 1024 * block : 1024 * (block + 1)], pick, preferred_element_type=F32)
            thinned[e, :, HD * block : HD * (block + 1)] = got.astype(BF16)

    def chunk(which, way, hops, part, n):
        back = hops if way == 0 else -hops
        if which == 0:
            return ga.at[wrap(z - back), pl.ds(HALF * part, HALF)]
        return gb.at[pl.ds(4 * part, 4), pl.ds(first_unit(wrap(x - back)), n)]

    def ring(which, way, hops, part, n):
        ref = chunk(which, way, hops, part, n)
        return remote(
            ref,
            ref,
            ring_send.at[which, way, hops, part],
            ring_recv.at[which, way, hops, part],
            neighbour(which, way),
        )

    def arrived(which, way, hops, part, n):
        ref = chunk(which, way, hops + 1, part, n)
        remote(
            ref, ref, ring_send.at[which, way, hops, part], ring_recv.at[which, way, hops, part], neighbour(which, way)
        ).wait_recv()

    def far_wide(way, hops):
        return lax.rem(wrap(x - (hops if way == 0 else -hops)), 4) == 3

    for hops in range(1, 4):
        for part in range(2):
            for way in range(2):
                goes_on = hops < 3 or part == way
                arrived(0, way, hops - 1, part, 0)
                if goes_on:
                    ring(0, way, hops, part, 0).start()

                def pass_column(n):
                    arrived(1, way, hops - 1, part, n)
                    if goes_on:
                        ring(1, way, hops, part, n).start()

                either(far_wide(way, hops), pass_column)
            thin(2 * (hops - 1) + part)
    thin(6)
    thin(7)
    for way in range(2):
        arrived(0, way, 3, way, 0)
        either(far_wide(way, 4), lambda n: arrived(1, way, 3, way, n))

    def tall(ref, first, units):
        flat = ref.reshape(SIDE * SLAB, 16, GRAIN)
        return flat[first : first + units].reshape(16 * units, GRAIN)

    both = jnp.concatenate([tall(ga, 0, QUERY_UNITS), tall(gb, 0, QUERY_UNITS)], axis=1)
    projected = jnp.dot(tokens[...], both, preferred_element_type=F32)
    narrow = jnp.zeros((4 * ROWS, 2 * HD), F32)
    for odd, ref in ((0, ga), (1, gb)):
        weight = jnp.concatenate(
            [tall(ref, QUERY_UNITS, KEY_UNITS), tall(ref, QUERY_UNITS + KEY_UNITS, KEY_UNITS)], axis=1
        )
        narrow += jnp.dot(thinned[4 * odd : 4 * odd + 4].reshape(4 * ROWS, D // 8), weight, preferred_element_type=F32)

    def folded(first):
        total = jnp.zeros((ROWS, HD), F32)
        for j in range(4):
            total += jnp.where(lane // 32 == j, narrow[ROWS * j : ROWS * (j + 1), first : first + HD], 0.0)
        total += pltpu.roll(total, 64, 1)
        return total + pltpu.roll(total, 32, 1)

    def placed(columns):
        other = pltpu.roll(columns, 16, 1)
        even = lax.rem(quarter, 2) == 0
        inside = lax.rem(lane, 64) // 16 == quarter
        straight = (lane < 64) == even
        return jnp.where(inside, jnp.where(straight, columns, other), 0.0)

    new_key, new_value = folded(0), folded(HD)
    new_key = new_key * tables[2] + pltpu.roll(new_key, 16, 1) * tables[3]
    tiles = []
    for head in range(2):
        part = projected[:, HD * head : HD * (head + 1)]
        tiles.append(part * tables[0] + pltpu.roll(part, 64, 1) * tables[1])
    tiles += [placed(new_key), placed(new_value)]
    for number, tile in enumerate(tiles):
        tile = tile.astype(BF16)
        for i in range(4):
            for s in range(2):
                outbox[i, number, 16 * s : 16 * s + 16] = tile[64 * s + 16 * i : 64 * s + 16 * i + 16]

    def swap(step, sending):
        target = lax.rem(quarter + step, 4)
        source = quarter if sending else lax.rem(quarter + 4 - step, 4)
        return remote(
            outbox.at[target], inbox.at[source], swap_send.at[step], swap_recv.at[step], (dp, t_base + target)
        )

    for step in range(1, 4):
        swap(step, True).start()
    inbox[quarter] = outbox[quarter]
    loads[2].wait()
    loads[3].wait()
    for step in range(1, 4):
        swap(step, False).wait_recv()

    for j in range(4):
        for head in range(2):
            for s in range(2):
                queries[pl.ds(8 * s + 2 * j + head, 16, stride=16), :] = inbox[j, head, 16 * s : 16 * s + 16].astype(F32)
    fresh = []
    for number in (2, 3):
        total = inbox[0, number].astype(F32)
        for j in range(1, 4):
            total += inbox[j, number].astype(F32)
        fresh.append(total.astype(BF16))
        for s in range(2):
            new_entries[s, :, HD * (number - 2) : HD * (number - 1)] = fresh[-1][16 * s : 16 * s + 16]
    empty = jnp.zeros((HD - 32, HD), BF16)
    fresh_keys, fresh_values = [jnp.concatenate([part, empty], axis=0) for part in fresh]
    asked = queries[...].astype(BF16)
    transposed = (((1,), (1,)), ((), ()))
    scale = HD**-0.5
    own = lax.dot_general(asked, fresh_keys, transposed, preferred_element_type=F32) * scale
    row, column = rows_of((256, HD)), lanes_of((256, HD))
    allowed = (lax.rem(column, 16) == row // 16) & (column // 16 <= lax.rem(row, 16) // 8)
    own = jnp.where(allowed, own, -1e30)
    scores = []
    for k in range(16):
        part = lax.dot_general(asked[16 * k : 16 * k + 16], keys[k], transposed, preferred_element_type=F32) * scale
        live = lanes_of((16, 256)) < lengths[0, quarter * 16 + k]
        scores.append(jnp.where(live, part, -1e30))
    scores = jnp.concatenate(scores, axis=0)
    top = jnp.maximum(jnp.max(scores, axis=1, keepdims=True), jnp.max(own, axis=1, keepdims=True))
    scores = jnp.exp(scores - top)
    own = jnp.exp(own - top)
    total = jnp.sum(scores, axis=1, keepdims=True) + jnp.sum(own, axis=1, keepdims=True)
    scores = scores.astype(BF16)
    parts = [
        jnp.dot(scores[16 * k : 16 * k + 16], values[k], preferred_element_type=F32) for k in range(16)
    ]
    result = jnp.concatenate(parts, axis=0) + jnp.dot(own.astype(BF16), fresh_values, preferred_element_type=F32)
    mixed[...] = result / total
    for s in range(2):
        for m in range(8):
            attended[s, :, HD * m : HD * (m + 1)] = mixed[pl.ds(8 * s + m, 16, stride=16), :].astype(BF16)

    @pl.when(dp < 63)
    def _():
        up.wait_send()

    @pl.when(dp > 0)
    def _():
        down.wait_send()

    def sent(n):
        for step in range(1, SIDE):
            light(0, step, n, True).wait_send()
            light(1, step, n, True).wait_send()
        for way in range(2):
            whole = ga.at[z]
            remote(whole, whole, ring_send.at[0, way, 0, 0], ring_recv.at[0, way, 0, 0], neighbour(0, way)).wait_send()
            whole = gb.at[:, pl.ds(first_unit(x), n)]
            remote(whole, whole, ring_send.at[1, way, 0, 0], ring_recv.at[1, way, 0, 0], neighbour(1, way)).wait_send()

    either(wide, sent)
    for way in range(2):
        for hops in range(1, 4):
            for part in range(2):
                if hops < 3 or part == way:
                    ring(0, way, hops, part, 0).wait_send()
                    either(far_wide(way, hops), lambda n: ring(1, way, hops, part, n).wait_send())
    for step in range(1, 4):
        swap(step, True).wait_send()


def per_device(masters, offsets, tokens, lengths, cache_keys, cache_values):
    any_space = pl.BlockSpec(memory_space=pltpu.HBM)
    scalars = pl.BlockSpec(memory_space=pltpu.SMEM)
    vector = pl.BlockSpec(memory_space=pltpu.VMEM)
    dma = pltpu.SemaphoreType.DMA
    mixed, fresh = pl.pallas_call(
        kernel,
        out_shape=(jax.ShapeDtypeStruct((2, 16, 1024), BF16), jax.ShapeDtypeStruct((2, 16, 256), BF16)),
        in_specs=[any_space, scalars, any_space, scalars, any_space, any_space],
        out_specs=(vector, vector),
        scratch_shapes=[
            pltpu.VMEM((528, GRAIN), F32),
            pltpu.VMEM((12, 2, 16, GRAIN), BF16),
            pltpu.VMEM((3, 2, 16, GRAIN), BF16),
            pltpu.VMEM((2, 2, 16, GRAIN), BF16),
            pltpu.VMEM((SIDE, SLAB, 16, GRAIN), BF16),
            pltpu.VMEM((SIDE, SLAB, 16, GRAIN), BF16),
            pltpu.VMEM((ROWS, D), BF16),
            pltpu.VMEM((16, 256, HD), BF16),
            pltpu.VMEM((16, 256, HD), BF16),
            pltpu.VMEM((8, ROWS, D // 8), BF16),
            pltpu.VMEM((ROWS, HD), F32),
            pltpu.VMEM((4, ROWS, HD), F32),
            pltpu.VMEM((4, 4, 32, HD), BF16),
            pltpu.VMEM((4, 4, 32, HD), BF16),
            pltpu.VMEM((256, HD), F32),
            pltpu.VMEM((256, HD), F32),
            dma((4,)),
            dma((2,)),
            dma((2,)),
            dma((2, SIDE)),
            dma((2, SIDE)),
            dma((2, 2, 4, 2)),
            dma((2, 2, 4, 2)),
            dma((4,)),
            dma((4,)),
        ],
        compiler_params=pltpu.CompilerParams(collective_id=0, has_side_effects=True, vmem_limit_bytes=40 * 2**20),
    )(
        masters.reshape(300, GRAIN),
        offsets,
        tokens.reshape(ROWS, D),
        lengths,
        cache_keys.reshape(16, 256, HD),
        cache_values.reshape(16, 256, HD),
    )
    return mixed.reshape(2, 1, 1, 16, 1024), fresh.reshape(2, 1, 1, 16, 256)


def solution(mesh):
    return jax.shard_map(
        per_device,
        mesh=mesh,
        in_specs=(
            P("tensor", "dp", None),
            P(),
            P(None, "dp", None, None),
            P("dp", None),
            P("dp", "tensor", None, None, None),
            P("dp", "tensor", None, None, None),
        ),
        out_specs=(P(None, "dp", "tensor", None, None), P(None, "dp", "tensor", None, None)),
        check_vma=False,
    )
```

```python
import math

import jax
import jax.numpy as jnp
from jax import lax
from jax.experimental import pallas as pl
from jax.experimental.pallas import tpu as pltpu
from jax.sharding import PartitionSpec as P

D = 5120
HD = 128
GRAIN = 128
SIDE = 8
UNIT = 32
SLAB = 50
HALF = SLAB // 2
QUERY_UNITS = 320
KEY_UNITS = 40
ROWS = 128
FRONT = 144
ROPE_BASE = 1000000.0
MESH = pl.DeviceIdType.MESH
F32 = jnp.float32
BF16 = jnp.bfloat16
NEAR_FIRST = (1, 7, 2, 6, 3, 5, 4)


def remote(src, dst, send_sem, recv_sem, device):
    return pltpu.make_async_remote_copy(
        src_ref=src, dst_ref=dst, send_sem=send_sem, recv_sem=recv_sem, device_id=device, device_id_type=MESH
    )


def wrap(value):
    return lax.rem(value + 2 * SIDE, SIDE)


def first_unit(x):
    return 6 * x + x // 4


def either(wide, act):
    @pl.when(wide)
    def _():
        act(7)

    @pl.when(jnp.logical_not(wide))
    def _():
        act(6)


def lanes_of(shape):
    return lax.broadcasted_iota(jnp.int32, shape, len(shape) - 1)


def rows_of(shape):
    return lax.broadcasted_iota(jnp.int32, shape, len(shape) - 2)


def kernel(
    masters,
    offsets,
    tokens_in,
    lengths,
    keys_in,
    values_in,
    attended,
    new_entries,
    raw,
    staged,
    from_below,
    from_above,
    ga,
    gb,
    tokens,
    keys,
    values,
    thinned,
    position,
    tables,
    outbox,
    inbox,
    queries,
    mixed,
    load_sem,
    near_send,
    near_recv,
    light_send,
    light_recv,
    ring_send,
    ring_recv,
    swap_send,
    swap_recv,
):
    dp = lax.axis_index("dp")
    t = lax.axis_index("tensor")
    z, x = dp // SIDE, lax.rem(dp, SIDE)
    quarter = lax.rem(t, 4)
    t_base = t - quarter

    loads = [
        pltpu.make_async_copy(masters.at[:, 0], raw.at[pl.ds(FRONT, 300)], load_sem.at[0]),
        pltpu.make_async_copy(tokens_in, tokens, load_sem.at[1]),
        pltpu.make_async_copy(keys_in, keys, load_sem.at[2]),
        pltpu.make_async_copy(values_in, values, load_sem.at[3]),
    ]
    for load in loads:
        load.start()

    barrier = pltpu.get_barrier_semaphore()
    for step in range(1, SIDE):
        pl.semaphore_signal(barrier, inc=1, device_id=(z * SIDE + wrap(x + step), t), device_id_type=MESH)
        pl.semaphore_signal(barrier, inc=1, device_id=(wrap(z + step) * SIDE + x, t), device_id_type=MESH)
    for step in range(1, 4):
        pl.semaphore_signal(barrier, inc=1, device_id=(dp, t_base + lax.rem(quarter + step, 4)), device_id_type=MESH)

    @pl.when(dp > 0)
    def _():
        pl.semaphore_signal(barrier, inc=1, device_id=(dp - 1, t), device_id_type=MESH)

    @pl.when(dp < 63)
    def _():
        pl.semaphore_signal(barrier, inc=1, device_id=(dp + 1, t), device_id_type=MESH)

    wide = lax.rem(x, 4) == 3
    count = jnp.where(wide, 7, 6)
    base = z * SLAB + first_unit(x)
    own_start = offsets[dp] // GRAIN
    own_end = offsets[dp + 1] // GRAIN
    raw[0:FRONT] = jnp.zeros((FRONT, GRAIN), F32)
    raw[FRONT + 300 : 528] = jnp.zeros((528 - FRONT - 300, GRAIN), F32)
    loads[0].wait()
    for w in range(12):
        begin = jnp.clip(FRONT + UNIT * (base - 2 + w) - own_start, 0, 494)
        for odd in range(2):
            staged[w, odd] = raw[pl.ds(begin + odd, 16, stride=2), :].astype(BF16)

    pl.semaphore_wait(barrier, 2 * (SIDE - 1) + 3 + jnp.where(dp > 0, 1, 0) + jnp.where(dp < 63, 1, 0))

    up = remote(
        staged.at[pl.ds(2 + count, 3)], from_below, near_send.at[0], near_recv.at[0], (jnp.minimum(dp + 1, 63), t)
    )
    down = remote(staged.at[pl.ds(0, 2)], from_above, near_send.at[1], near_recv.at[1], (jnp.maximum(dp - 1, 0), t))

    @pl.when(dp < 63)
    def _():
        up.start()

    @pl.when(dp > 0)
    def _():
        down.start()

    @pl.when(dp > 0)
    def _():
        up.wait_recv()

    @pl.when(dp < 63)
    def _():
        down.wait_recv()

    def settle(i):
        for odd, target in ((0, ga), (1, gb)):
            row = UNIT * (base + i) + odd + 2 * rows_of((16, GRAIN))
            entry = staged[2 + i, odd].astype(F32)
            if i < 3:
                entry = jnp.where(row < own_start, from_below[i, odd].astype(F32), entry)
            if i > 3:
                place = jnp.clip(i - count + 2, 0, 1)
                entry = jnp.where(row >= own_end, from_above[place, odd].astype(F32), entry)
            target[z, first_unit(x) + i] = entry.astype(BF16)

    for i in range(6):
        settle(i)

    @pl.when(wide)
    def _():
        settle(6)

    def piece(ref, at_z, at_x, n):
        return ref.at[at_z, pl.ds(first_unit(at_x), n)]

    def light(which, step, n, sending):
        if which == 0:
            other = wrap(x + step)
            at_x = x if sending else wrap(x - step)
            ref = piece(ga, z, at_x, n)
            device = (z * SIDE + other, t)
        else:
            at_z = z if sending else wrap(z - step)
            ref = piece(gb, at_z, x, n)
            device = (wrap(z + step) * SIDE + x, t)
        return remote(ref, ref, light_send.at[which, step], light_recv.at[which, step], device)

    def neighbour(which, way):
        move = 1 if way == 0 else -1
        return (wrap(z + move) * SIDE + x, t) if which == 0 else (z * SIDE + wrap(x + move), t)

    def spread(which, at, n):
        for way in range(2):
            ref = piece(ga, z, at, n) if which == 0 else piece(gb, at, x, n)
            remote(
                ref, ref, ring_send.at[which, way, 0, 0], ring_recv.at[which, way, 0, at // 4], neighbour(which, way)
            ).start()

    def send_own(n):
        spread(0, x, n)
        spread(1, z, n)
        for step in NEAR_FIRST:
            light(0, step, n, True).start()
            light(1, step, n, True).start()

    either(wide, send_own)

    for r in range(64):
        here = jnp.full((1, HD), lengths[0, r], jnp.int32).astype(F32)
        position[r : r + 1] = here
        position[64 + r : 65 + r] = here + 1.0
    lane = lanes_of((ROWS, HD))
    rate = -2.0 * math.log(ROPE_BASE) / HD
    angle = position[...] * jnp.exp(lax.rem(lane, 64).astype(F32) * rate)
    tables[0] = jnp.cos(angle)
    tables[1] = jnp.where(lane < 64, -1.0, 1.0) * jnp.sin(angle)
    angle = position[...] * jnp.exp((quarter * 16 + lax.rem(lane, 16)).astype(F32) * rate)
    tables[2] = jnp.cos(angle)
    tables[3] = jnp.where(lax.rem(lane, 32) < 16, -1.0, 1.0) * jnp.sin(angle)

    for step in NEAR_FIRST:
        at_x = wrap(x - step)

        def pass_a(n):
            light(0, step, n, False).wait_recv()
            spread(0, at_x, n)

        def pass_b(n):
            light(1, step, n, False).wait_recv()
            spread(1, wrap(z - step), n)

        either(lax.rem(at_x, 4) == 3, pass_a)
        either(wide, pass_b)

    loads[1].wait()

    def thin(e):
        pick = (rows_of((1024, HD)) == 8 * lanes_of((1024, HD)) + e).astype(F32).astype(BF16)
        for block in range(D // 1024):
            got = jnp.dot(tokens[:, 1024 * block : 1024 * (block + 1)], pick, preferred_element_type=F32)
            thinned[e, :, HD * block : HD * (block + 1)] = got.astype(BF16)

    def chunk(which, way, hops, part, n):
        back = hops if way == 0 else -hops
        if which == 0:
            return ga.at[wrap(z - back), pl.ds(HALF * part, HALF)]
        return gb.at[pl.ds(4 * part, 4), pl.ds(first_unit(wrap(x - back)), n)]

    def ring(which, way, hops, part, n):
        ref = chunk(which, way, hops, part, n)
        return remote(
            ref,
            ref,
            ring_send.at[which, way, hops, part],
            ring_recv.at[which, way, hops, part],
            neighbour(which, way),
        )

    def arrived(which, way, hops, part, n):
        ref = chunk(which, way, hops + 1, part, n)
        remote(
            ref, ref, ring_send.at[which, way, hops, part], ring_recv.at[which, way, hops, part], neighbour(which, way)
        ).wait_recv()

    def far_wide(way, hops):
        return lax.rem(wrap(x - (hops if way == 0 else -hops)), 4) == 3

    for hops in range(1, 4):
        for part in range(2):
            for way in range(2):
                goes_on = hops < 3 or part == way
                arrived(0, way, hops - 1, part, 0)
                if goes_on:
                    ring(0, way, hops, part, 0).start()

                def pass_column(n):
                    arrived(1, way, hops - 1, part, n)
                    if goes_on:
                        ring(1, way, hops, part, n).start()

                either(far_wide(way, hops), pass_column)
            thin(2 * (hops - 1) + part)
    thin(6)
    thin(7)
    for way in range(2):
        arrived(0, way, 3, way, 0)
        either(far_wide(way, 4), lambda n: arrived(1, way, 3, way, n))

    def tall(ref, first, units):
        flat = ref.reshape(SIDE * SLAB, 16, GRAIN)
        return flat[first : first + units].reshape(16 * units, GRAIN)

    both = jnp.concatenate([tall(ga, 0, QUERY_UNITS), tall(gb, 0, QUERY_UNITS)], axis=1)
    projected = jnp.dot(tokens[...], both, preferred_element_type=F32)
    narrow = jnp.zeros((4 * ROWS, 2 * HD), F32)
    for odd, ref in ((0, ga), (1, gb)):
        weight = jnp.concatenate(
            [tall(ref, QUERY_UNITS, KEY_UNITS), tall(ref, QUERY_UNITS + KEY_UNITS, KEY_UNITS)], axis=1
        )
        narrow += jnp.dot(thinned[4 * odd : 4 * odd + 4].reshape(4 * ROWS, D // 8), weight, preferred_element_type=F32)

    def folded(first):
        total = jnp.zeros((ROWS, HD), F32)
        for j in range(4):
            total += jnp.where(lane // 32 == j, narrow[ROWS * j : ROWS * (j + 1), first : first + HD], 0.0)
        total += pltpu.roll(total, 64, 1)
        return total + pltpu.roll(total, 32, 1)

    def placed(columns):
        other = pltpu.roll(columns, 16, 1)
        even = lax.rem(quarter, 2) == 0
        inside = lax.rem(lane, 64) // 16 == quarter
        straight = (lane < 64) == even
        return jnp.where(inside, jnp.where(straight, columns, other), 0.0)

    new_key, new_value = folded(0), folded(HD)
    new_key = new_key * tables[2] + pltpu.roll(new_key, 16, 1) * tables[3]
    tiles = []
    for head in range(2):
        part = projected[:, HD * head : HD * (head + 1)]
        tiles.append(part * tables[0] + pltpu.roll(part, 64, 1) * tables[1])
    tiles += [placed(new_key), placed(new_value)]
    for number, tile in enumerate(tiles):
        tile = tile.astype(BF16)
        for i in range(4):
            for s in range(2):
                outbox[i, number, 16 * s : 16 * s + 16] = tile[64 * s + 16 * i : 64 * s + 16 * i + 16]

    def swap(step, sending):
        target = lax.rem(quarter + step, 4)
        source = quarter if sending else lax.rem(quarter + 4 - step, 4)
        return remote(
            outbox.at[target], inbox.at[source], swap_send.at[step], swap_recv.at[step], (dp, t_base + target)
        )

    for step in range(1, 4):
        swap(step, True).start()
    inbox[quarter] = outbox[quarter]
    loads[2].wait()
    loads[3].wait()
    for step in range(1, 4):
        swap(step, False).wait_recv()

    for j in range(4):
        for head in range(2):
            for s in range(2):
                queries[pl.ds(8 * s + 2 * j + head, 16, stride=16), :] = inbox[j, head, 16 * s : 16 * s + 16].astype(F32)
    fresh = []
    for number in (2, 3):
        total = inbox[0, number].astype(F32)
        for j in range(1, 4):
            total += inbox[j, number].astype(F32)
        fresh.append(total.astype(BF16))
        for s in range(2):
            new_entries[s, :, HD * (number - 2) : HD * (number - 1)] = fresh[-1][16 * s : 16 * s + 16]
    empty = jnp.zeros((HD - 32, HD), BF16)
    fresh_keys, fresh_values = [jnp.concatenate([part, empty], axis=0) for part in fresh]
    asked = queries[...].astype(BF16)
    transposed = (((1,), (1,)), ((), ()))
    scale = HD**-0.5
    own = lax.dot_general(asked, fresh_keys, transposed, preferred_element_type=F32) * scale
    row, column = rows_of((256, HD)), lanes_of((256, HD))
    allowed = (lax.rem(column, 16) == row // 16) & (column // 16 <= lax.rem(row, 16) // 8)
    own = jnp.where(allowed, own, -1e30)
    scores = []
    for k in range(16):
        part = lax.dot_general(asked[16 * k : 16 * k + 16], keys[k], transposed, preferred_element_type=F32) * scale
        live = lanes_of((16, 256)) < lengths[0, quarter * 16 + k]
        scores.append(jnp.where(live, part, -1e30))
    scores = jnp.concatenate(scores, axis=0)
    top = jnp.maximum(jnp.max(scores, axis=1, keepdims=True), jnp.max(own, axis=1, keepdims=True))
    scores = jnp.exp(scores - top)
    own = jnp.exp(own - top)
    total = jnp.sum(scores, axis=1, keepdims=True) + jnp.sum(own, axis=1, keepdims=True)
    scores = scores.astype(BF16)
    parts = [
        jnp.dot(scores[16 * k : 16 * k + 16], values[k], preferred_element_type=F32) for k in range(16)
    ]
    result = jnp.concatenate(parts, axis=0) + jnp.dot(own.astype(BF16), fresh_values, preferred_element_type=F32)
    mixed[...] = result / total
    for s in range(2):
        for m in range(8):
            attended[s, :, HD * m : HD * (m + 1)] = mixed[pl.ds(8 * s + m, 16, stride=16), :].astype(BF16)

    @pl.when(dp < 63)
    def _():
        up.wait_send()

    @pl.when(dp > 0)
    def _():
        down.wait_send()

    def sent(n):
        for step in range(1, SIDE):
            light(0, step, n, True).wait_send()
            light(1, step, n, True).wait_send()
        for way in range(2):
            whole = ga.at[z]
            remote(whole, whole, ring_send.at[0, way, 0, 0], ring_recv.at[0, way, 0, 0], neighbour(0, way)).wait_send()
            whole = gb.at[:, pl.ds(first_unit(x), n)]
            remote(whole, whole, ring_send.at[1, way, 0, 0], ring_recv.at[1, way, 0, 0], neighbour(1, way)).wait_send()

    either(wide, sent)
    for way in range(2):
        for hops in range(1, 4):
            for part in range(2):
                if hops < 3 or part == way:
                    ring(0, way, hops, part, 0).wait_send()
                    either(far_wide(way, hops), lambda n: ring(1, way, hops, part, n).wait_send())
    for step in range(1, 4):
        swap(step, True).wait_send()


def per_device(masters, offsets, tokens, lengths, cache_keys, cache_values):
    any_space = pl.BlockSpec(memory_space=pltpu.HBM)
    scalars = pl.BlockSpec(memory_space=pltpu.SMEM)
    vector = pl.BlockSpec(memory_space=pltpu.VMEM)
    dma = pltpu.SemaphoreType.DMA
    mixed, fresh = pl.pallas_call(
        kernel,
        out_shape=(jax.ShapeDtypeStruct((2, 16, 1024), BF16), jax.ShapeDtypeStruct((2, 16, 256), BF16)),
        in_specs=[any_space, scalars, any_space, scalars, any_space, any_space],
        out_specs=(vector, vector),
        scratch_shapes=[
            pltpu.VMEM((528, GRAIN), F32),
            pltpu.VMEM((12, 2, 16, GRAIN), BF16),
            pltpu.VMEM((3, 2, 16, GRAIN), BF16),
            pltpu.VMEM((2, 2, 16, GRAIN), BF16),
            pltpu.VMEM((SIDE, SLAB, 16, GRAIN), BF16),
            pltpu.VMEM((SIDE, SLAB, 16, GRAIN), BF16),
            pltpu.VMEM((ROWS, D), BF16),
            pltpu.VMEM((16, 256, HD), BF16),
            pltpu.VMEM((16, 256, HD), BF16),
            pltpu.VMEM((8, ROWS, D // 8), BF16),
            pltpu.VMEM((ROWS, HD), F32),
            pltpu.VMEM((4, ROWS, HD), F32),
            pltpu.VMEM((4, 4, 32, HD), BF16),
            pltpu.VMEM((4, 4, 32, HD), BF16),
            pltpu.VMEM((256, HD), F32),
            pltpu.VMEM((256, HD), F32),
            dma((4,)),
            dma((2,)),
            dma((2,)),
            dma((2, SIDE)),
            dma((2, SIDE)),
            dma((2, 2, 4, 2)),
            dma((2, 2, 4, 2)),
            dma((4,)),
            dma((4,)),
        ],
        compiler_params=pltpu.CompilerParams(collective_id=0, has_side_effects=True, vmem_limit_bytes=60 * 2**20),
    )(
        masters.reshape(300, 1, GRAIN),
        offsets,
        tokens.reshape(ROWS, D),
        lengths,
        cache_keys.reshape(16, 256, HD),
        cache_values.reshape(16, 256, HD),
    )
    return mixed.reshape(2, 1, 1, 16, 1024), fresh.reshape(2, 1, 1, 16, 256)


def solution(mesh):
    return jax.shard_map(
        per_device,
        mesh=mesh,
        in_specs=(
            P("tensor", "dp", None),
            P(),
            P(None, "dp", None, None),
            P("dp", None),
            P("dp", "tensor", None, None, None),
            P("dp", "tensor", None, None, None),
        ),
        out_specs=(P(None, "dp", "tensor", None, None), P(None, "dp", "tensor", None, None)),
        check_vma=False,
    )
```
